256 devices in a mesh: ka: 16 (over y, z_hi, core), ga: 16 (over z_lo, x).
Axes of the slice: x: 4, y: 4, z: 8 (z_hi: 2, z_lo: 4; z = z_hi * 4 + z_lo), core: 2. Of those that a mesh axis runs over, the one named last changes fastest.
Arguments:
- bands: bfloat16 [32, 2, 512, 32768], P('ka', None, None, 'ga'), may hold values from -1.5 to 1.5
- nbr_slot: int32 [32], P('ka'), may hold values from 0 to 1, as said below
- gshift: int32 [32], P('ka'), may hold values from -1 to 1
Outputs:
- margin: float32 [512, 32, 2, 512], P('ga', 'ka')
The draws below stay inside these ranges and needn't reach their ends.
Inputs may be any that keep to these rules, and one draw needn't show every extreme that they name: `nbr_slot`: for the 2 k-points of one group the entries are a permutation of 0 to 1.
All inputs are finite; a program needn't handle non-finite values.
Results may differ from the reference program's by a relative error of at most 0.0028.
Values may be sent and summed in bfloat16 or wider, within the bound.
A program may use at most 128 MiB of HBM per device.

```python
import math
import jax
import jax.numpy as jnp
from jax import lax

NB = 512
K_DEV = 2
NKB = 4
X_DEV = 2
PLANE = 1024
NX = 32
NPTS = 32768
KPTS = 32
N_KA = 16
N_GA = 16


def draw_nbr_slot(key, part):
    key = jax.random.fold_in(key, 7)
    group_keys = jax.random.split(key, KPTS // K_DEV)
    orders = jax.vmap(lambda single: jax.random.permutation(single, K_DEV))(group_keys)
    return orders.reshape(KPTS).astype(jnp.int32)


def with_ends(values, key, smallest, top_value):
    longest = values.shape.index(max(values.shape))
    spots = []
    for shift in (0, 1):
        where = [jax.random.randint(jax.random.fold_in(key, axis), (), 0, length) for axis, length in enumerate(values.shape)]
        where[longest] = (where[longest] + shift) % values.shape[longest]
        spots.append(tuple(where))
    return values.at[spots[0]].set(smallest).at[spots[1]].set(top_value)


def with_spikes(values, stream_key, source, target, shards_of, factor):
    def block_of(position):
        return (jnp.arange(values.shape[position]) // (values.shape[position] // shards_of)).reshape((-1,) + (1,) * (values.ndim - 1 - position))

    one_side = jax.random.permutation(stream_key, shards_of)[block_of(target)]
    far = (block_of(target) + shards_of // 2) % shards_of
    return jnp.where((block_of(source) == one_side) | (block_of(source) == far), factor * values, values)


def level_of(stream_key, shape, pieces, least, high):
    def one(position, blocks):
        heights = jax.random.uniform(jax.random.fold_in(jax.random.fold_in(stream_key, 6), position), (blocks,), jnp.float32, least / len(pieces), high / len(pieces))
        return jnp.repeat(jnp.exp(heights), shape[position] // blocks).reshape((-1,) + (1,) * (len(shape) - position - 1))

    gain = one(*pieces[0])
    for cut in pieces[1:]:
        gain = gain * one(*cut)
    return gain


def gaussian_with(own_key, dims, deviation, bound, cuts, heavy, held_as=jnp.bfloat16):
    values = deviation * jax.random.normal(own_key, dims, jnp.float32)
    if cuts:
        values = values * level_of(own_key, dims, cuts, -0.22, 0.18)
    return jnp.clip(with_spikes(values, jax.random.fold_in(own_key, 3), *heavy), -bound, bound).astype(held_as)


def setup_inputs(seed: int = 0) -> dict:
    splits = jax.random.split(jax.random.key(seed), 4)
    return {
        "bands": gaussian_with(splits[0], (KPTS, 2, NB, NPTS), (1.0 / (X_DEV * PLANE * N_GA) ** 0.25), 1.5, ((0, 16), (3, 16)), (3, 2, 16, 2.0)),
        "nbr_slot": draw_nbr_slot(jax.random.fold_in(splits[3], 71), 0),
        "gshift": with_ends(jax.random.randint(splits[2], (KPTS,), -1, 2), jax.random.fold_in(splits[2], 1), -1, 1).astype(jnp.int32),
    }


def phase_field(slab, shift_g):
    planes = jnp.arange(NPTS, dtype=jnp.int32) // PLANE
    turns = ((1 + NKB * shift_g) * planes) % (NKB * NX)
    angle = (2.0 * math.pi / (NKB * NX)) * turns.astype(jnp.float32)
    cosine = jnp.cos(angle)
    sine = jnp.sin(angle)
    real_part = slab[0].astype(jnp.float32)
    imag_part = slab[1].astype(jnp.float32)
    near_re = real_part * cosine + imag_part * sine
    near_im = imag_part * cosine - real_part * sine
    return jnp.stack([near_re, near_im]).astype(jnp.bfloat16)


def margin_one(conj_side, near):
    terms = jnp.einsum("cmx,dnx->cdmn", conj_side.astype(jnp.float32), near.astype(jnp.float32))
    real_part = terms[0, 0] + terms[1, 1]
    imag_part = terms[0, 1] - terms[1, 0]
    return jnp.stack([real_part, imag_part])


def reference(bands, nbr_slot, gshift):
    def one_point(kidx):
        group = kidx // K_DEV
        slot = lax.dynamic_index_in_dim(nbr_slot, kidx, 0, keepdims=False)
        other = (((group + 1) % N_KA) * K_DEV + slot).astype(jnp.int32)
        conj_side = lax.dynamic_index_in_dim(bands, kidx, 0, keepdims=False)
        partner = lax.dynamic_index_in_dim(bands, other, 0, keepdims=False)
        shift_g = lax.dynamic_index_in_dim(gshift, kidx, 0, keepdims=False)
        return margin_one(conj_side, phase_field(partner, shift_g))

    result = lax.map(one_point, jnp.arange(KPTS, dtype=jnp.int32))
    return jnp.transpose(result, (2, 0, 1, 3))
```

```python
import math

import jax
import jax.numpy as jnp
from jax import lax
from jax.experimental import pallas as pl
from jax.experimental.pallas import tpu as pltpu
from jax.sharding import PartitionSpec as P

NKB = 4
PLANE = 1024
NX_DEV = 4
CHUNKS = 8
MESH = pl.DeviceIdType.MESH


def kernel(
    slot_ref, shift_ref, bands, out_ref,
    own, there, trig, near, part, xbuf, zsend, zbuf, result,
    own_sem, send_sem, recv_sem, xsend_sem, xrecv_sem, zsend_sem, zrecv_sem,
):
    ka, ga = lax.axis_index("ka"), lax.axis_index("ga")
    n_ka, n_ga = lax.axis_size("ka"), lax.axis_size("ga")
    n_x = NX_DEV
    n_z = n_ga // n_x
    z, x = ga // n_x, lax.rem(ga, n_x)
    chunks, cols = there.shape[0], there.shape[3]
    kpts, points = there.shape[1], there.shape[4]
    rows = out_ref.shape[2]
    total_planes = points // PLANE * n_ga

    before = lax.rem(ka + n_ka - 1, n_ka)
    after = lax.rem(ka + 1, n_ka)

    def along_x(d):
        return z * n_x + lax.rem(x + d + n_x, n_x)

    def along_z(d):
        return lax.rem(z + d + n_z, n_z) * n_x + x

    fetch = pltpu.make_async_copy(bands, own, own_sem)
    fetch.start()

    barrier = pltpu.get_barrier_semaphore()
    greeted = [(before, ga), (after, ga)]
    greeted += [(ka, along_x(d)) for d in range(1, n_x)]
    greeted += [(ka, along_z(d)) for d in range(1, n_z)]
    for device in greeted:
        pl.semaphore_signal(barrier, inc=1, device_id=device, device_id_type=MESH)
    pl.semaphore_wait(barrier, len(greeted))

    def slab_copy(c):
        return pltpu.make_async_remote_copy(
            src_ref=bands.at[:, :, pl.ds(c * cols, cols), :],
            dst_ref=there.at[c],
            send_sem=send_sem.at[c],
            recv_sem=recv_sem.at[c],
            device_id=(before, ga),
            device_id_type=MESH,
        )

    def x_copy(c, d):
        return pltpu.make_async_remote_copy(
            src_ref=part.at[c, :, :, lax.rem(x + d, n_x)],
            dst_ref=xbuf.at[c, d - 1],
            send_sem=xsend_sem.at[c, d - 1],
            recv_sem=xrecv_sem.at[c, d - 1],
            device_id=(ka, along_x(d)),
            device_id_type=MESH,
        )

    def z_copy(c, d):
        return pltpu.make_async_remote_copy(
            src_ref=zsend.at[c, d - 1],
            dst_ref=zbuf.at[c, d - 1],
            send_sem=zsend_sem.at[c, d - 1],
            recv_sem=zrecv_sem.at[c, d - 1],
            device_id=(ka, along_z(d)),
            device_id_type=MESH,
        )

    @pl.loop(0, chunks)
    def _(c):
        slab_copy(c).start()

    plane = ga * (points // PLANE) + lax.broadcasted_iota(jnp.int32, (1, points), 1) // PLANE
    for k in range(kpts):
        turns = (1 + NKB * shift_ref[k]) * plane % (NKB * total_planes)
        angle = 2.0 * math.pi / (NKB * total_planes) * turns.astype(jnp.float32)
        trig[k, 0:1] = jnp.cos(angle)
        trig[k, 1:2] = jnp.sin(angle)

    fetch.wait()

    def multiply(c):
        slab_copy(c).wait_recv()

        @pl.loop(0, cols // 16)
        def _(step):
            lo = pl.multiple_of(step * 16, 16)
            for k in range(kpts):
                first = slot_ref[k] == 0
                re = jnp.where(first, there[c, 0, 0, pl.ds(lo, 16), :], there[c, 1, 0, pl.ds(lo, 16), :]).astype(jnp.float32)
                im = jnp.where(first, there[c, 0, 1, pl.ds(lo, 16), :], there[c, 1, 1, pl.ds(lo, 16), :]).astype(jnp.float32)
                cosine, sine = trig[k, 0:1], trig[k, 1:2]
                near_re = (re * cosine + im * sine).astype(jnp.bfloat16)
                near_im = (im * cosine - re * sine).astype(jnp.bfloat16)
                near[k, 0, pl.ds(lo, 16), :] = near_re
                near[k, 0, pl.ds(cols + lo, 16), :] = near_im
                near[k, 1, pl.ds(lo, 16), :] = near_im
                near[k, 1, pl.ds(cols + lo, 16), :] = -near_re

        @pl.loop(0, kpts)
        def _(k):
            over_points = (((1,), (1,)), ((), ()))
            terms = lax.dot_general(own[k, 0], near[k, 0], over_points, preferred_element_type=jnp.float32)
            terms += lax.dot_general(own[k, 1], near[k, 1], over_points, preferred_element_type=jnp.float32)
            part[c, k] = terms.reshape(part.shape[2:])

        for d in range(1, n_x):
            x_copy(c, d).start()

    def sum_x(c):
        for d in range(1, n_x):
            x_copy(c, d).wait_recv()

        def at(zz):
            total = part[c, :, zz, x]
            for d in range(1, n_x):
                total += xbuf[c, d - 1, :, zz]
            return total

        for d in range(1, n_z):
            zsend[c, d - 1] = at(lax.rem(z + d, n_z)).astype(jnp.bfloat16)
            z_copy(c, d).start()
        result[c] = at(z)

    def sum_z(c):
        for d in range(1, n_z):
            z_copy(c, d).wait_recv()
        total = result[c]
        for d in range(1, n_z):
            total += zbuf[c, d - 1].astype(jnp.float32)
        result[c] = total

    @pl.loop(0, chunks)
    def _(c):
        multiply(c)

        @pl.when(c >= 1)
        def _():
            sum_x(c - 1)

        @pl.when(c >= 2)
        def _():
            sum_z(c - 2)

    sum_x(chunks - 1)
    sum_z(chunks - 2)
    sum_z(chunks - 1)

    for k in range(kpts):
        for half in range(2):
            pieces = [result[c, k][:, half * cols : (half + 1) * cols] for c in range(chunks)]
            out_ref[k, half] = jnp.concatenate(pieces, axis=1)

    @pl.loop(0, chunks)
    def _(c):
        slab_copy(c).wait_send()
        for d in range(1, n_x):
            x_copy(c, d).wait_send()
        for d in range(1, n_z):
            z_copy(c, d).wait_send()


def body(bands, nbr_slot, gshift):
    kpts, _, nbands, points = bands.shape
    n_x = NX_DEV
    n_ga = lax.axis_size("ga")
    n_z = n_ga // n_x
    rows = nbands // n_ga
    cols = nbands // CHUNKS
    out = pl.pallas_call(
        kernel,
        name="margins",
        out_shape=jax.ShapeDtypeStruct((kpts, 2, rows, nbands), jnp.float32),
        in_specs=[
            pl.BlockSpec(memory_space=pltpu.SMEM),
            pl.BlockSpec(memory_space=pltpu.SMEM),
            pl.BlockSpec(memory_space=pl.ANY),
        ],
        out_specs=pl.BlockSpec(memory_space=pltpu.VMEM),
        scratch_shapes=[
            pltpu.VMEM((kpts, 2, nbands, points), jnp.bfloat16),
            pltpu.VMEM((CHUNKS, kpts, 2, cols, points), jnp.bfloat16),
            pltpu.VMEM((kpts, 2, points), jnp.float32),
            pltpu.VMEM((kpts, 2, 2 * cols, points), jnp.bfloat16),
            pltpu.VMEM((CHUNKS, kpts, n_z, n_x, rows, 2 * cols), jnp.float32),
            pltpu.VMEM((CHUNKS, n_x - 1, kpts, n_z, rows, 2 * cols), jnp.float32),
            pltpu.VMEM((CHUNKS, n_z - 1, kpts, rows, 2 * cols), jnp.bfloat16),
            pltpu.VMEM((CHUNKS, n_z - 1, kpts, rows, 2 * cols), jnp.bfloat16),
            pltpu.VMEM((CHUNKS, kpts, rows, 2 * cols), jnp.float32),
            pltpu.SemaphoreType.DMA,
            pltpu.SemaphoreType.DMA((CHUNKS,)),
            pltpu.SemaphoreType.DMA((CHUNKS,)),
            pltpu.SemaphoreType.DMA((CHUNKS, n_x - 1)),
            pltpu.SemaphoreType.DMA((CHUNKS, n_x - 1)),
            pltpu.SemaphoreType.DMA((CHUNKS, n_z - 1)),
            pltpu.SemaphoreType.DMA((CHUNKS, n_z - 1)),
        ],
        compiler_params=pltpu.CompilerParams(
            collective_id=0, has_side_effects=True, vmem_limit_bytes=48 * 1024 * 1024
        ),
    )(nbr_slot, gshift, bands)
    return jnp.transpose(out, (2, 0, 1, 3))


def solution(mesh):
    placed = (P("ka", None, None, "ga"), P("ka"), P("ka"))
    return jax.shard_map(
        body, mesh=mesh, in_specs=placed, out_specs=P("ga", "ka", None, None), check_vma=False
    )
```

```python
import contextlib
import math

import jax
import jax.numpy as jnp
from jax import lax
from jax.experimental import pallas as pl
from jax.experimental.pallas import tpu as pltpu
from jax.sharding import PartitionSpec as P

NKB = 4
PLANE = 1024
N_X = 4
CHUNKS = 16
DEPTH = 3
TILE = 16
LANES = 128
LAG = 3
MESH = pl.DeviceIdType.MESH
OVER_POINTS = (((1,), (1,)), ((), ()))


def scope(name):
    return contextlib.nullcontext()


def kernel(
    slot_hbm, shift_hbm, bands, out_ref,
    slot_ref, shift_ref, own, there, trig, near, part, xbuf, zsend, zmid, zbuf, last_send, last_buf, result,
    own_sem, small_sem, pace_sem, core_sem, recv_sem, xsend_sem, xrecv_sem, zsend_sem, zmid_sem, zrecv_sem,
    last_send_sem, last_recv_sem,
):
    ka, ga = lax.axis_index("ka"), lax.axis_index("ga")
    n_ka, n_ga = lax.axis_size("ka"), lax.axis_size("ga")
    n_x = N_X
    n_z = n_ga // n_x
    z, x = ga // n_x, lax.rem(ga, n_x)
    core = lax.rem(ka, 2)
    pieces, kpts, _, cols, _ = there.shape
    chunks = part.shape[0]
    halves = pieces // chunks
    points = own.shape[3]
    total_planes = points // PLANE * n_ga

    before = lax.rem(ka + n_ka - 1, n_ka)
    after = lax.rem(ka + 1, n_ka)

    others = [(dz, dx) for dz in range(n_z) for dx in range(n_x) if dz or dx]

    def relative(dz, dx):
        return lax.rem(z + dz, n_z) * n_x + lax.rem(x + dx, n_x)

    fetch = pltpu.make_async_copy(bands, own, own_sem)
    fetch.start()
    small = [
        pltpu.make_async_copy(slot_hbm, slot_ref, small_sem.at[0]),
        pltpu.make_async_copy(shift_hbm, shift_ref, small_sem.at[1]),
    ]
    for copy in small:
        copy.start()

    barrier = pltpu.get_barrier_semaphore()
    greeted = [(before, ga), (after, ga)]
    greeted += [(ka, relative(*away)) for away in others]
    for device in greeted:
        pl.semaphore_signal(barrier, inc=1, device_id=device, device_id_type=MESH)
    with scope("barrier"):
        pl.semaphore_wait(barrier, len(greeted))

    def slab_copy(p, sem):
        c, h = p // halves, lax.rem(p, halves)
        rows = pl.ds(pl.multiple_of(c * cols, cols), cols)
        lanes = pl.ds(pl.multiple_of(h * PLANE, PLANE), PLANE)
        return pltpu.make_async_remote_copy(
            src_ref=bands.at[:, :, rows, lanes],
            dst_ref=there.at[p],
            send_sem=sem,
            recv_sem=recv_sem.at[p],
            device_id=(before, ga),
            device_id_type=MESH,
        )

    def x_copy(c, d):
        return pltpu.make_async_remote_copy(
            src_ref=part.at[c, :, lax.rem(x + d, n_x)],
            dst_ref=xbuf.at[c, d - 1],
            send_sem=xsend_sem,
            recv_sem=xrecv_sem.at[c],
            device_id=(ka, relative(0, d)),
            device_id_type=MESH,
        )

    inward = jnp.where(z < n_z // 2, 1, -1)
    outer = (z == 0) | (z == n_z - 1)

    def to_inner(c):
        return pltpu.make_async_remote_copy(
            src_ref=zsend.at[c],
            dst_ref=zmid.at[c],
            send_sem=zsend_sem,
            recv_sem=zmid_sem.at[c],
            device_id=(ka, ga + inward * n_x),
            device_id_type=MESH,
        )

    def from_inner(c, j):
        far = (-1, 1, 2)[j]
        return pltpu.make_async_remote_copy(
            src_ref=zsend.at[c, j],
            dst_ref=zbuf.at[c, 0 if j else 1],
            send_sem=zsend_sem,
            recv_sem=zrecv_sem.at[c],
            device_id=(ka, ga + far * inward * n_x),
            device_id_type=MESH,
        )

    def last_copy(dz, dx):
        return pltpu.make_async_remote_copy(
            src_ref=last_send.at[lax.rem(z + dz, n_z), lax.rem(x + dx, n_x)],
            dst_ref=last_buf.at[dz * n_x + dx],
            send_sem=last_send_sem,
            recv_sem=last_recv_sem,
            device_id=(ka, relative(dz, dx)),
            device_id_type=MESH,
        )

    def wait_for(ref, sem):
        pltpu.make_async_copy(ref, ref, sem).wait()

    @pl.when(core == 1)
    def _():
        @pl.loop(0, pieces)
        def _(p):
            slab_copy(p, core_sem).start()

    @pl.when(core == 0)
    def _():
        @pl.loop(0, DEPTH)
        def _(p):
            slab_copy(p, pace_sem.at[p]).start()

    for copy in small:
        copy.wait()
    plane = ga * (points // PLANE) + lax.broadcasted_iota(jnp.int32, (1, points), 1) // PLANE
    for k in range(kpts):
        turns = (1 + NKB * shift_ref[k]) * plane % (NKB * total_planes)
        angle = 2.0 * math.pi / (NKB * total_planes) * turns.astype(jnp.float32)
        trig[k, 0:1] = jnp.cos(angle)
        trig[k, 1:2] = jnp.sin(angle)

    near[...] = jnp.zeros_like(near)

    fetch.wait()

    def multiply(p):
        c, h = p // halves, lax.rem(p, halves)
        lanes = pl.ds(pl.multiple_of(h * PLANE, PLANE), PLANE)
        with scope("slab"):
            wait_for(there.at[p], recv_sem.at[p])

        @pl.loop(0, cols // TILE)
        def _(step):
            lo = pl.multiple_of(step * TILE, TILE)
            rows = pl.ds(lo, TILE)
            re_0, im_0, re_1, im_1 = (there[p, k, part_, rows, :] for k in range(kpts) for part_ in range(2))
            for k in range(kpts):
                first = slot_ref[k] == 0
                re = jnp.where(first, re_0, re_1).astype(jnp.float32)
                im = jnp.where(first, im_0, im_1).astype(jnp.float32)
                cosine, sine = trig[k, 0:1, lanes], trig[k, 1:2, lanes]
                near_re = (re * cosine + im * sine).astype(jnp.bfloat16)
                near_im = (im * cosine - re * sine).astype(jnp.bfloat16)
                upper = pl.ds(2 * k * cols + lo, TILE)
                lower = pl.ds((2 * k + 1) * cols + lo, TILE)
                near[k, 0, upper, :] = near_re
                near[k, 0, lower, :] = near_im
                near[k, 1, upper, :] = near_im
                near[k, 1, lower, :] = -near_re

        terms = None
        for k in range(kpts):
            for half in range(2):
                term = lax.dot_general(
                    own[k, half, :, lanes], near[k, half], OVER_POINTS, preferred_element_type=jnp.float32
                )
                terms = term if terms is None else terms + term
        terms = terms.reshape(part.shape[1:])

        @pl.when(h == 0)
        def _():
            part[c] = terms

        @pl.when(h > 0)
        def _():
            part[c] += terms

        @pl.when((h == halves - 1) & (c < chunks - 1))
        def _():
            for d in range(1, n_x):
                x_copy(c, d).start()

        @pl.when((h == halves - 1) & (c == chunks - 1))
        def _():
            last_send[...] = part[c].astype(jnp.bfloat16)
            for away in others:
                last_copy(*away).start()

    def over_x(c, zz):
        total = part[c, zz, x]
        for d in range(1, n_x):
            total += xbuf[c, d - 1, zz]
        return total

    def sum_x(c):
        with scope("sumx"):
            wait_for(xbuf.at[c], xrecv_sem.at[c])

        @pl.when(outer)
        def _():
            for j in range(n_z - 1):
                zsend[c, j] = over_x(c, z + (j + 1) * inward).astype(jnp.bfloat16)
            to_inner(c).start()

        @pl.when(jnp.logical_not(outer))
        def _():
            zsend[c, 0] = over_x(c, z - inward).astype(jnp.bfloat16)
            from_inner(c, 0).start()

        result[c] = over_x(c, z)

    def sum_inner(c):
        @pl.when(jnp.logical_not(outer))
        def _():
            with scope("inner"):
                wait_for(zmid.at[c], zmid_sem.at[c])
            for j in (1, 2):
                total = over_x(c, z + j * inward) + zmid[c, j].astype(jnp.float32)
                zsend[c, j] = total.astype(jnp.bfloat16)
                from_inner(c, j).start()
            result[c] += zmid[c, 0].astype(jnp.float32)

    def sum_z(c):
        @pl.when(outer)
        def _():
            with scope("sumz"):
                wait_for(zbuf.at[c], zrecv_sem.at[c])
            result[c] += zbuf[c, 0].astype(jnp.float32) + zbuf[c, 1].astype(jnp.float32)

        @pl.when(jnp.logical_not(outer))
        def _():
            with scope("sumz"):
                wait_for(zbuf.at[c, 0], zrecv_sem.at[c])
            result[c] += zbuf[c, 0].astype(jnp.float32)

    @pl.loop(0, pieces)
    def _(i):
        @pl.when((core == 0) & (i >= DEPTH))
        def _():
            sem = pace_sem.at[lax.rem(i, DEPTH)]
            with scope("pace"):
                wait_for(there.at[i], sem)
            slab_copy(i, sem).start()

        first = jnp.where(core == 0, jnp.minimum(halves * i, pieces), i)
        last = jnp.where(core == 0, jnp.minimum(halves * i + halves, pieces), i + 1)

        @pl.loop(first, last)
        def _(p):
            multiply(p)

        whole = (core == 0) | (lax.rem(i, halves) == halves - 1)
        c = jnp.where(core == 0, i, i // halves)
        lag = jnp.where(core == 0, 2 * LAG, LAG)

        @pl.when(whole & (c >= 1) & (c < chunks))
        def _():
            sum_x(c - 1)

        @pl.when(whole & (c > lag) & (c - lag < chunks))
        def _():
            sum_inner(c - lag - 1)

    @pl.loop(jnp.where(core == 0, chunks - 1, chunks - LAG - 1), chunks - 1)
    def _(c):
        sum_inner(c)

    @pl.loop(0, chunks - 1)
    def _(c):
        sum_z(c)

    with scope("last"):
        wait_for(last_buf.at[pl.ds(1, n_z * n_x - 1)], last_recv_sem)
    total = part[chunks - 1, z, x]
    for dz, dx in others:
        total += last_buf[dz * n_x + dx].astype(jnp.float32)
    result[chunks - 1] = total

    blocks = chunks * cols // LANES
    rows = result.shape[1]
    for k in range(kpts):
        for half in range(2):
            lo = (2 * k + half) * cols
            for b in range(blocks):
                members = range(b * chunks // blocks, (b + 1) * chunks // blocks)
                block = jnp.concatenate([result[c][:, lo : lo + cols] for c in members], axis=1)
                out_ref[pl.ds((k * blocks + b) * 2 + half, rows, stride=kpts * blocks * 2), :] = block

    with scope("end"):
        @pl.when(core == 1)
        def _():
            wait_for(there, core_sem)

        @pl.when(core == 0)
        def _():
            @pl.loop(0, DEPTH)
            def _(p):
                wait_for(there.at[p], pace_sem.at[p])

        wait_for(xbuf, xsend_sem)
        wait_for(zsend, zsend_sem)
        wait_for(last_buf.at[pl.ds(1, n_z * n_x - 1)], last_send_sem)


def body(bands, nbr_slot, gshift):
    kpts, _, nbands, points = bands.shape
    n_x = N_X
    n_ga = lax.axis_size("ga")
    n_z = n_ga // n_x
    rows = nbands // n_ga
    cols = nbands // CHUNKS
    lanes = 2 * kpts * cols
    pieces = CHUNKS * (points // PLANE)
    out = pl.pallas_call(
        kernel,
        name="margins",
        out_shape=jax.ShapeDtypeStruct((rows * kpts * 2 * nbands // LANES, LANES), jnp.float32),
        in_specs=[
            pl.BlockSpec(memory_space=pltpu.HBM),
            pl.BlockSpec(memory_space=pltpu.HBM),
            pl.BlockSpec(memory_space=pl.ANY),
        ],
        out_specs=pl.BlockSpec(memory_space=pltpu.VMEM),
        scratch_shapes=[
            pltpu.SMEM((kpts,), jnp.int32),
            pltpu.SMEM((kpts,), jnp.int32),
            pltpu.VMEM((kpts, 2, nbands, points), jnp.bfloat16),
            pltpu.VMEM((pieces, kpts, 2, cols, PLANE), jnp.bfloat16),
            pltpu.VMEM((kpts, 2, points), jnp.float32),
            pltpu.VMEM((kpts, 2, lanes, PLANE), jnp.bfloat16),
            pltpu.VMEM((CHUNKS, n_z, n_x, rows, lanes), jnp.float32),
            pltpu.VMEM((CHUNKS - 1, n_x - 1, n_z, rows, lanes), jnp.float32),
            pltpu.VMEM((CHUNKS - 1, n_z - 1, rows, lanes), jnp.bfloat16),
            pltpu.VMEM((CHUNKS - 1, n_z - 1, rows, lanes), jnp.bfloat16),
            pltpu.VMEM((CHUNKS - 1, 2, rows, lanes), jnp.bfloat16),
            pltpu.VMEM((n_z, n_x, rows, lanes), jnp.bfloat16),
            pltpu.VMEM((n_z * n_x, rows, lanes), jnp.bfloat16),
            pltpu.VMEM((CHUNKS, rows, lanes), jnp.float32),
            pltpu.SemaphoreType.DMA,
            pltpu.SemaphoreType.DMA((2,)),
            pltpu.SemaphoreType.DMA((DEPTH,)),
            pltpu.SemaphoreType.DMA,
            pltpu.SemaphoreType.DMA((pieces,)),
            pltpu.SemaphoreType.DMA,
            pltpu.SemaphoreType.DMA((CHUNKS - 1,)),
            pltpu.SemaphoreType.DMA,
            pltpu.SemaphoreType.DMA((CHUNKS - 1,)),
            pltpu.SemaphoreType.DMA((CHUNKS - 1,)),
            pltpu.SemaphoreType.DMA,
            pltpu.SemaphoreType.DMA,
        ],
        compiler_params=pltpu.CompilerParams(
            collective_id=0, has_side_effects=True, vmem_limit_bytes=63 * 1024 * 1024
        ),
    )(nbr_slot, gshift, bands)
    out = out.reshape(rows, kpts, nbands // LANES, 2, LANES)
    return jnp.transpose(out, (0, 1, 3, 2, 4)).reshape(rows, kpts, 2, nbands)


def solution(mesh):
    placed = (P("ka", None, None, "ga"), P("ka"), P("ka"))
    return jax.shard_map(
        body, mesh=mesh, in_specs=placed, out_specs=P("ga", "ka", None, None), check_vma=False
    )
```

```python
import contextlib
import math

import jax
import jax.numpy as jnp
from jax import lax
from jax.experimental import pallas as pl
from jax.experimental.pallas import tpu as pltpu
from jax.sharding import PartitionSpec as P

NKB = 4
PLANE = 1024
N_X = 4
CHUNKS = 16
DEPTH = 3
TILE = 16
LANES = 128
LAG = 3
MESH = pl.DeviceIdType.MESH
OVER_POINTS = (((1,), (1,)), ((), ()))


def scope(name):
    return contextlib.nullcontext()


def kernel(
    slot_hbm, shift_hbm, bands, out_ref,
    slot_ref, shift_ref, own, there, trig, near, part, xbuf, zsend, zmid, zbuf, last_send, last_buf, result,
    own_sem, small_sem, pace_sem, core_sem, recv_sem, xsend_sem, xrecv_sem, zsend_sem, zmid_sem, zrecv_sem,
    last_send_sem, last_recv_sem,
):
    ka, ga = lax.axis_index("ka"), lax.axis_index("ga")
    n_ka, n_ga = lax.axis_size("ka"), lax.axis_size("ga")
    n_x = N_X
    n_z = n_ga // n_x
    z, x = ga // n_x, lax.rem(ga, n_x)
    core = lax.rem(ka, 2)
    pieces, kpts, _, cols, _ = there.shape
    chunks = part.shape[0]
    halves = pieces // chunks
    points = own.shape[3]
    total_planes = points // PLANE * n_ga

    before = lax.rem(ka + n_ka - 1, n_ka)
    after = lax.rem(ka + 1, n_ka)

    others = [(dz, dx) for dz in range(n_z) for dx in range(n_x) if dz or dx]

    def relative(dz, dx):
        return lax.rem(z + dz, n_z) * n_x + lax.rem(x + dx, n_x)

    fetch = pltpu.make_async_copy(bands, own, own_sem)
    fetch.start()
    small = [
        pltpu.make_async_copy(slot_hbm, slot_ref, small_sem.at[0]),
        pltpu.make_async_copy(shift_hbm, shift_ref, small_sem.at[1]),
    ]
    for copy in small:
        copy.start()

    barrier = pltpu.get_barrier_semaphore()
    greeted = [(before, ga), (after, ga)]
    greeted += [(ka, relative(*away)) for away in others]
    for device in greeted:
        pl.semaphore_signal(barrier, inc=1, device_id=device, device_id_type=MESH)
    with scope("barrier"):
        pl.semaphore_wait(barrier, len(greeted))

    def slab_copy(p, sem):
        c, h = p // halves, lax.rem(p, halves)
        rows = pl.ds(pl.multiple_of(c * cols, cols), cols)
        lanes = pl.ds(pl.multiple_of(h * PLANE, PLANE), PLANE)
        return pltpu.make_async_remote_copy(
            src_ref=bands.at[:, :, rows, lanes],
            dst_ref=there.at[p],
            send_sem=sem,
            recv_sem=recv_sem.at[p],
            device_id=(before, ga),
            device_id_type=MESH,
        )

    def x_copy(c, d):
        return pltpu.make_async_remote_copy(
            src_ref=part.at[c, :, lax.rem(x + d, n_x)],
            dst_ref=xbuf.at[c, d - 1],
            send_sem=xsend_sem,
            recv_sem=xrecv_sem.at[c],
            device_id=(ka, relative(0, d)),
            device_id_type=MESH,
        )

    inward = jnp.where(z < n_z // 2, 1, -1)
    outer = (z == 0) | (z == n_z - 1)

    def to_inner(c):
        return pltpu.make_async_remote_copy(
            src_ref=zsend.at[c],
            dst_ref=zmid.at[c],
            send_sem=zsend_sem,
            recv_sem=zmid_sem.at[c],
            device_id=(ka, ga + inward * n_x),
            device_id_type=MESH,
        )

    def from_inner(c, j):
        far = (-1, 1, 2)[j]
        return pltpu.make_async_remote_copy(
            src_ref=zsend.at[c, j],
            dst_ref=zbuf.at[c, 0 if j else 1],
            send_sem=zsend_sem,
            recv_sem=zrecv_sem.at[c],
            device_id=(ka, ga + far * inward * n_x),
            device_id_type=MESH,
        )

    def last_copy(dz, dx):
        return pltpu.make_async_remote_copy(
            src_ref=last_send.at[lax.rem(z + dz, n_z), lax.rem(x + dx, n_x)],
            dst_ref=last_buf.at[dz * n_x + dx],
            send_sem=last_send_sem,
            recv_sem=last_recv_sem,
            device_id=(ka, relative(dz, dx)),
            device_id_type=MESH,
        )

    def wait_for(ref, sem):
        pltpu.make_async_copy(ref, ref, sem).wait()

    @pl.when(core == 1)
    def _():
        @pl.loop(0, pieces)
        def _(p):
            slab_copy(p, core_sem).start()

    @pl.when(core == 0)
    def _():
        @pl.loop(0, DEPTH)
        def _(p):
            slab_copy(p, pace_sem.at[p]).start()

    for copy in small:
        copy.wait()
    plane = ga * (points // PLANE) + lax.broadcasted_iota(jnp.int32, (1, points), 1) // PLANE
    for k in range(kpts):
        turns = (1 + NKB * shift_ref[k]) * plane % (NKB * total_planes)
        angle = 2.0 * math.pi / (NKB * total_planes) * turns.astype(jnp.float32)
        trig[k, 0:1] = jnp.cos(angle)
        trig[k, 1:2] = jnp.sin(angle)

    near[...] = jnp.zeros_like(near)

    fetch.wait()

    def multiply(p):
        c, h = p // halves, lax.rem(p, halves)
        lanes = pl.ds(pl.multiple_of(h * PLANE, PLANE), PLANE)
        with scope("slab"):
            wait_for(there.at[p], recv_sem.at[p])

        @pl.loop(0, cols // TILE)
        def _(step):
            lo = pl.multiple_of(step * TILE, TILE)
            rows = pl.ds(lo, TILE)
            re_0, im_0, re_1, im_1 = (there[p, k, part_, rows, :] for k in range(kpts) for part_ in range(2))
            for k in range(kpts):
                first = slot_ref[k] == 0
                re = jnp.where(first, re_0, re_1).astype(jnp.float32)
                im = jnp.where(first, im_0, im_1).astype(jnp.float32)
                cosine, sine = trig[k, 0:1, lanes], trig[k, 1:2, lanes]
                near_re = (re * cosine + im * sine).astype(jnp.bfloat16)
                near_im = (im * cosine - re * sine).astype(jnp.bfloat16)
                upper = pl.ds(2 * k * cols + lo, TILE)
                lower = pl.ds((2 * k + 1) * cols + lo, TILE)
                near[k, 0, upper, :] = near_re
                near[k, 0, lower, :] = near_im
                near[k, 1, upper, :] = near_im
                near[k, 1, lower, :] = -near_re

        terms = None
        for k in range(kpts):
            for half in range(2):
                term = lax.dot_general(
                    own[k, half, :, lanes], near[k, half], OVER_POINTS, preferred_element_type=jnp.float32
                )
                terms = term if terms is None else terms + term
        terms = terms.reshape(part.shape[1:])

        @pl.when(h == 0)
        def _():
            part[c] = terms

        @pl.when(h > 0)
        def _():
            part[c] += terms

        @pl.when((h == halves - 1) & (c < chunks - 1))
        def _():
            for d in range(1, n_x):
                x_copy(c, d).start()

        @pl.when((h == halves - 1) & (c == chunks - 1))
        def _():
            last_send[...] = part[c].astype(jnp.bfloat16)
            for away in others:
                last_copy(*away).start()

    def over_x(c, zz):
        total = part[c, zz, x]
        for d in range(1, n_x):
            total += xbuf[c, d - 1, zz]
        return total

    def sum_x(c):
        with scope("sumx"):
            wait_for(xbuf.at[c], xrecv_sem.at[c])

        @pl.when(outer)
        def _():
            for j in range(n_z - 1):
                zsend[c, j] = over_x(c, z + (j + 1) * inward).astype(jnp.bfloat16)
            to_inner(c).start()

        @pl.when(jnp.logical_not(outer))
        def _():
            zsend[c, 0] = over_x(c, z - inward).astype(jnp.bfloat16)
            from_inner(c, 0).start()

        result[c] = over_x(c, z)

    def sum_inner(c):
        @pl.when(jnp.logical_not(outer))
        def _():
            with scope("inner"):
                wait_for(zmid.at[c], zmid_sem.at[c])
            for j in (1, 2):
                total = over_x(c, z + j * inward) + zmid[c, j].astype(jnp.float32)
                zsend[c, j] = total.astype(jnp.bfloat16)
                from_inner(c, j).start()
            result[c] += zmid[c, 0].astype(jnp.float32)

    def sum_z(c):
        @pl.when(outer)
        def _():
            with scope("sumz"):
                wait_for(zbuf.at[c], zrecv_sem.at[c])
            result[c] += zbuf[c, 0].astype(jnp.float32) + zbuf[c, 1].astype(jnp.float32)

        @pl.when(jnp.logical_not(outer))
        def _():
            with scope("sumz"):
                wait_for(zbuf.at[c, 0], zrecv_sem.at[c])
            result[c] += zbuf[c, 0].astype(jnp.float32)

    @pl.loop(0, pieces)
    def _(i):
        @pl.when((core == 0) & (i >= DEPTH))
        def _():
            sem = pace_sem.at[lax.rem(i, DEPTH)]
            with scope("pace"):
                wait_for(there.at[i], sem)
            slab_copy(i, sem).start()

        first = jnp.where(core == 0, jnp.minimum(halves * i, pieces), i)
        last = jnp.where(core == 0, jnp.minimum(halves * i + halves, pieces), i + 1)

        @pl.loop(first, last)
        def _(p):
            multiply(p)

        whole = (core == 0) | (lax.rem(i, halves) == 0)
        c = jnp.where(core == 0, i, i // halves)
        lag = jnp.where(core == 0, 2 * LAG, LAG)

        @pl.when(whole & (c >= 1) & (c < chunks))
        def _():
            sum_x(c - 1)

        @pl.when(whole & (c > lag) & (c - lag < chunks))
        def _():
            sum_inner(c - lag - 1)

    @pl.loop(jnp.where(core == 0, chunks - 1, chunks - LAG - 1), chunks - 1)
    def _(c):
        sum_inner(c)

    @pl.loop(0, chunks - 1)
    def _(c):
        sum_z(c)

    with scope("last"):
        wait_for(last_buf.at[pl.ds(1, n_z * n_x - 1)], last_recv_sem)
    total = part[chunks - 1, z, x]
    for dz, dx in others:
        total += last_buf[dz * n_x + dx].astype(jnp.float32)
    result[chunks - 1] = total

    blocks = chunks * cols // LANES
    rows = result.shape[1]
    for k in range(kpts):
        for half in range(2):
            lo = (2 * k + half) * cols
            for b in range(blocks):
                members = range(b * chunks // blocks, (b + 1) * chunks // blocks)
                block = jnp.concatenate([result[c][:, lo : lo + cols] for c in members], axis=1)
                out_ref[pl.ds((k * blocks + b) * 2 + half, rows, stride=kpts * blocks * 2), :] = block

    with scope("end"):
        @pl.when(core == 1)
        def _():
            wait_for(there, core_sem)

        @pl.when(core == 0)
        def _():
            @pl.loop(0, DEPTH)
            def _(p):
                wait_for(there.at[p], pace_sem.at[p])

        wait_for(xbuf, xsend_sem)
        wait_for(zsend, zsend_sem)
        wait_for(last_buf.at[pl.ds(1, n_z * n_x - 1)], last_send_sem)


def body(bands, nbr_slot, gshift):
    kpts, _, nbands, points = bands.shape
    n_x = N_X
    n_ga = lax.axis_size("ga")
    n_z = n_ga // n_x
    rows = nbands // n_ga
    cols = nbands // CHUNKS
    lanes = 2 * kpts * cols
    pieces = CHUNKS * (points // PLANE)
    out = pl.pallas_call(
        kernel,
        name="margins",
        out_shape=jax.ShapeDtypeStruct((rows * kpts * 2 * nbands // LANES, LANES), jnp.float32),
        in_specs=[
            pl.BlockSpec(memory_space=pltpu.HBM),
            pl.BlockSpec(memory_space=pltpu.HBM),
            pl.BlockSpec(memory_space=pl.ANY),
        ],
        out_specs=pl.BlockSpec(memory_space=pltpu.VMEM),
        scratch_shapes=[
            pltpu.SMEM((kpts,), jnp.int32),
            pltpu.SMEM((kpts,), jnp.int32),
            pltpu.VMEM((kpts, 2, nbands, points), jnp.bfloat16),
            pltpu.VMEM((pieces, kpts, 2, cols, PLANE), jnp.bfloat16),
            pltpu.VMEM((kpts, 2, points), jnp.float32),
            pltpu.VMEM((kpts, 2, lanes, PLANE), jnp.bfloat16),
            pltpu.VMEM((CHUNKS, n_z, n_x, rows, lanes), jnp.float32),
            pltpu.VMEM((CHUNKS - 1, n_x - 1, n_z, rows, lanes), jnp.float32),
            pltpu.VMEM((CHUNKS - 1, n_z - 1, rows, lanes), jnp.bfloat16),
            pltpu.VMEM((CHUNKS - 1, n_z - 1, rows, lanes), jnp.bfloat16),
            pltpu.VMEM((CHUNKS - 1, 2, rows, lanes), jnp.bfloat16),
            pltpu.VMEM((n_z, n_x, rows, lanes), jnp.bfloat16),
            pltpu.VMEM((n_z * n_x, rows, lanes), jnp.bfloat16),
            pltpu.VMEM((CHUNKS, rows, lanes), jnp.float32),
            pltpu.SemaphoreType.DMA,
            pltpu.SemaphoreType.DMA((2,)),
            pltpu.SemaphoreType.DMA((DEPTH,)),
            pltpu.SemaphoreType.DMA,
            pltpu.SemaphoreType.DMA((pieces,)),
            pltpu.SemaphoreType.DMA,
            pltpu.SemaphoreType.DMA((CHUNKS - 1,)),
            pltpu.SemaphoreType.DMA,
            pltpu.SemaphoreType.DMA((CHUNKS - 1,)),
            pltpu.SemaphoreType.DMA((CHUNKS - 1,)),
            pltpu.SemaphoreType.DMA,
            pltpu.SemaphoreType.DMA,
        ],
        compiler_params=pltpu.CompilerParams(
            collective_id=0, has_side_effects=True, vmem_limit_bytes=63 * 1024 * 1024
        ),
    )(nbr_slot, gshift, bands)
    out = out.reshape(rows, kpts, nbands // LANES, 2, LANES)
    return jnp.transpose(out, (0, 1, 3, 2, 4)).reshape(rows, kpts, 2, nbands)


def solution(mesh):
    placed = (P("ka", None, None, "ga"), P("ka"), P("ka"))
    return jax.shard_map(
        body, mesh=mesh, in_specs=placed, out_specs=P("ga", "ka", None, None), check_vma=False
    )
```
